32 devices in a mesh: grp: 2 (over x), stn: 8 (over z, y), chan: 2 (over core).
Axes of the slice: x: 2, y: 2, z: 4, core: 2. Of those that a mesh axis runs over, the one named last changes fastest.
Arguments:
- voltage: bfloat16 [2, 32, 1048576], P(None, ('grp', 'stn'), 'chan'), parts along dimension 1, may hold values from -6 to 6
- earlier_samples: bfloat16 [2, 32, 61440], P(None, ('grp', 'stn')), parts along dimension 1, may hold values from -6 to 6
- prototype: float32 [16, 4096], replicated, may hold values from -1.5 to 1.5
Outputs:
- visibilities: float32 [2, 8192, 256], P(None, ('grp', 'stn', 'chan')), parts along dimension 1
The draws below stay inside these ranges and needn't reach their ends.
There are 2 independent parts, one for each index of `grp`. The reference program is written for one: setup_inputs(seed, part) draws one part's arguments, and reference() takes and returns one part's arrays. A program takes and returns all parts, laid end to end along the dimension named above; an argument that names none is the same for every part. Nothing has to cross between parts.
All inputs are finite; a program needn't handle non-finite values.
Results may differ from the reference program's by a relative error of at most 0.0044.
Values may be sent and summed in bfloat16 or wider, within the bound.
A program may use at most 64 MiB of HBM per device.

```python
import math
import jax
import jax.numpy as jnp
from jax import lax

NCH = 4096
FA = 64
FB = 64
TAPS = 16
INPUTS = 16
SPEC = 256


def shard_levels(own_key, extent, cuts, smallest, largest):
    loudness, own = 1.0, jax.random.fold_in(own_key, 6)
    for position, parts in cuts:
        steps = jnp.exp(jax.random.uniform(jax.random.fold_in(own, position), (parts,), jnp.float32, smallest / len(cuts), largest / len(cuts)))
        loudness = loudness * jnp.repeat(steps, extent[position] // parts).reshape([-1 if axis == position else 1 for axis in range(len(extent))])
    return loudness


def bell_draw(rng, extent, width, limit, pieces=(), dtype=jnp.bfloat16):
    drawn = jax.random.normal(rng, extent, jnp.float32) * width
    if len(pieces) > 0:
        drawn = shard_levels(rng, extent, pieces, -0.22, 0.18) * drawn
    return jnp.clip(drawn, min=-limit, max=limit).astype(dtype)


def setup_inputs(seed: int = 0, part: int = 0) -> dict:
    key_of = jax.random.split(jax.random.key(seed), 4)
    own_keys = jax.random.split(jax.random.fold_in(key_of[3], part), 4)
    voltage = bell_draw(own_keys[0], (2, INPUTS, SPEC * NCH), 1.0, 6.0, ((1, 8), (2, 2)))
    earlier_samples = bell_draw(own_keys[1], (2, INPUTS, (TAPS - 1) * NCH), 1.0, 6.0, ((1, 8),))
    prototype = bell_draw(key_of[2], (TAPS, NCH), TAPS ** -0.5, 1.5, (), jnp.float32)
    return {"voltage": voltage, "earlier_samples": earlier_samples, "prototype": prototype}


def small_tables(length):
    row_index = lax.broadcasted_iota(jnp.int32, (length, length), 0)
    col_index = lax.broadcasted_iota(jnp.int32, (length, length), 1)
    phase_angle = ((row_index * col_index) % length).astype(jnp.float32) * (2.0 * math.pi / length)
    return jnp.cos(phase_angle).astype(jnp.bfloat16), jnp.sin(phase_angle).astype(jnp.bfloat16)


def reference(voltage, earlier_samples, prototype):
    stream = jnp.concatenate([earlier_samples, voltage], axis=2).astype(jnp.float32)
    frames = stream.reshape(2, INPUTS, SPEC + TAPS - 1, NCH)
    filtered = jnp.zeros((2, INPUTS, SPEC, NCH), jnp.float32)
    for tap_number in range(TAPS):
        filtered = filtered + prototype[tap_number].astype(jnp.float32) * frames[:, :, tap_number:tap_number + SPEC]
    rounded = lax.optimization_barrier(filtered.astype(jnp.bfloat16))
    factored = rounded.astype(jnp.float32).reshape(2, INPUTS * SPEC, FA, FB)
    first_cos, first_sin = small_tables(FA)
    second_cos, second_sin = small_tables(FB)
    high = lax.Precision.HIGHEST
    with_cos = jnp.einsum("crab,ak->crkb", factored, first_cos.astype(jnp.float32), precision=high)
    with_sin = jnp.einsum("crab,ak->crkb", factored, first_sin.astype(jnp.float32), precision=high)
    g_real = with_cos[0] + with_sin[1]
    g_imag = with_cos[1] - with_sin[0]
    row_k = lax.broadcasted_iota(jnp.int32, (FA, FB), 0)
    col_b = lax.broadcasted_iota(jnp.int32, (FA, FB), 1)
    twist = ((row_k * col_b) % NCH).astype(jnp.float32) * (2.0 * math.pi / NCH)
    twist_cos = jnp.cos(twist)
    twist_sin = jnp.sin(twist)
    inner = jnp.stack([g_real * twist_cos + g_imag * twist_sin, g_imag * twist_cos - g_real * twist_sin])
    inner = lax.optimization_barrier(inner.astype(jnp.bfloat16)).astype(jnp.float32)
    second_a = jnp.einsum("crkb,bm->crkm", inner, second_cos.astype(jnp.float32), precision=high)
    second_b = jnp.einsum("crkb,bm->crkm", inner, second_sin.astype(jnp.float32), precision=high)
    scale_factor = NCH ** -0.5
    real_part = (second_a[0] + second_b[1]) * scale_factor
    imag_part = (second_a[1] - second_b[0]) * scale_factor
    ordered = jnp.transpose(jnp.stack([real_part, imag_part]), (0, 1, 3, 2))
    spectra = ordered.astype(jnp.bfloat16).reshape(2, INPUTS, SPEC, NCH)
    block_size = math.gcd(NCH, 512)
    channel_major = jnp.moveaxis(spectra.reshape(2, INPUTS, SPEC, NCH // block_size, block_size), 3, 0)

    def correlate(panel):
        wide = panel.astype(jnp.float32)
        products = jnp.einsum("xisc,yjsc->xycij", wide, wide, precision=high)
        real_sum = products[0, 0] + products[1, 1]
        imag_sum = products[1, 0] - products[0, 1]
        return jnp.stack([real_sum, imag_sum]) / SPEC

    blocks = lax.map(correlate, channel_major)
    return jnp.transpose(blocks, (1, 0, 2, 3, 4)).reshape(2, NCH, INPUTS * INPUTS)
```

```python
import functools
import math

import jax
import jax.numpy as jnp
import numpy as np
from jax import lax
from jax.experimental import pallas as pl
from jax.experimental.pallas import tpu as pltpu
from jax.sharding import PartitionSpec as P

FA = 64
LANES = 128
SUB = 8
PACK = 16
GROUPS = 4
MESH = pl.DeviceIdType.MESH


def passed_along(block, axis, distance):
    devices = range(lax.axis_size(axis))
    route = [(i - distance, i) for i in devices if i - distance in devices]
    return lax.ppermute(block, axis, route)


def small_tables(length):
    row_index = lax.broadcasted_iota(jnp.int32, (length, length), 0)
    col_index = lax.broadcasted_iota(jnp.int32, (length, length), 1)
    phase_angle = (row_index * col_index % length).astype(jnp.float32) * (2.0 * math.pi / length)
    return (jnp.cos(phase_angle).astype(jnp.bfloat16), jnp.sin(phase_angle).astype(jnp.bfloat16))


def general_shards(voltage, earlier_samples, prototype):
    components, local_inputs, samples = voltage.shape
    tap_count, channels = prototype.shape
    spectra_here = samples // channels
    frames = voltage.reshape(components, local_inputs, spectra_here, channels)
    tail_frames = frames[:, :, spectra_here - (tap_count - 1) :]
    passed = passed_along(tail_frames, "chan", 1)
    earlier = earlier_samples.reshape(components, local_inputs, tap_count - 1, channels)
    leading = lax.axis_index("chan") == 0
    history = jnp.where(leading, earlier, passed)
    stacked = jnp.concatenate([history, frames], axis=2)
    filtered = jnp.zeros((components, local_inputs, spectra_here, channels), jnp.float32)
    for tap_number in range(tap_count):
        window_frames = stacked[:, :, tap_number : tap_number + spectra_here].astype(jnp.float32)
        filtered = filtered + prototype[tap_number] * window_frames
    half_rows = local_inputs * spectra_here
    first_factor = FA
    second_factor = channels // first_factor
    factored = filtered.astype(jnp.bfloat16).reshape(
        components, half_rows, first_factor, second_factor
    )
    first_cos, first_sin = small_tables(first_factor)
    second_cos, second_sin = small_tables(second_factor)
    with_cos = jnp.einsum("crab,ak->crkb", factored, first_cos, preferred_element_type=jnp.float32)
    with_sin = jnp.einsum("crab,ak->crkb", factored, first_sin, preferred_element_type=jnp.float32)
    g_real = with_cos[0] + with_sin[1]
    g_imag = with_cos[1] - with_sin[0]
    row_k = lax.broadcasted_iota(jnp.int32, (first_factor, second_factor), 0)
    col_b = lax.broadcasted_iota(jnp.int32, (first_factor, second_factor), 1)
    twist = (row_k * col_b % channels).astype(jnp.float32) * (2.0 * math.pi / channels)
    twist_cos = jnp.cos(twist)
    twist_sin = jnp.sin(twist)
    inner = jnp.stack(
        [g_real * twist_cos + g_imag * twist_sin, g_imag * twist_cos - g_real * twist_sin]
    ).astype(jnp.bfloat16)
    second_a = jnp.einsum("crkb,bm->crkm", inner, second_cos, preferred_element_type=jnp.float32)
    second_b = jnp.einsum("crkb,bm->crkm", inner, second_sin, preferred_element_type=jnp.float32)
    scale_factor = channels ** (-0.5)
    real_part = (second_a[0] + second_b[1]) * scale_factor
    imag_part = (second_a[1] - second_b[0]) * scale_factor
    ordered = jnp.transpose(jnp.stack([real_part, imag_part]), (0, 1, 3, 2))
    spectra = ordered.astype(jnp.bfloat16).reshape(components, local_inputs, spectra_here, channels)
    station_count = lax.axis_size("stn")
    core_count = lax.axis_size("chan")
    owners = station_count * core_count
    owned = channels // owners
    shaped = spectra.reshape(components, local_inputs, spectra_here, owners, owned)
    moved = lax.all_to_all(shaped, ("stn", "chan"), split_axis=3, concat_axis=3, tiled=True)
    moved = moved.reshape(components, local_inputs, spectra_here, station_count, core_count, owned)
    moved = jnp.transpose(moved, (0, 3, 1, 4, 2, 5)).reshape(
        components, station_count * local_inputs, core_count * spectra_here, owned
    )
    all_inputs = moved.shape[1]
    spectra_total = moved.shape[2]
    products = jnp.einsum("xisc,yjsc->xycij", moved, moved, preferred_element_type=jnp.float32)
    real_sum = products[0, 0] + products[1, 1]
    imag_sum = products[1, 0] - products[0, 1]
    averaged = jnp.stack([real_sum, imag_sum]) / spectra_total
    return averaged.reshape(components, owned, all_inputs * all_inputs)


def tables(channels, owners, rows, inputs):
    q_count = channels // LANES
    q = np.arange(q_count)
    lane = np.arange(LANES)
    ang1 = 2.0 * np.pi * (np.outer(q, q) % q_count) / q_count
    cos1, sin1 = np.cos(ang1), np.sin(ang1)
    one = np.block([[cos1, sin1], [-sin1, cos1]])
    one = one.reshape(2, q_count, 2, q_count)
    eye = np.eye(SUB)
    first = np.einsum("ckdq,st->ckstdq", one, eye).reshape(2 * q_count * SUB, SUB * 2 * q_count)
    ang = 2.0 * np.pi * (np.outer(q, lane) % channels) / channels
    twist_cos, twist_sin = np.cos(ang), np.sin(ang)
    ang2 = 2.0 * np.pi * (np.outer(lane, lane) % LANES) / LANES
    scale = channels ** -0.5
    cos2, sin2 = np.cos(ang2) * scale, np.sin(ang2) * scale
    two = np.stack([np.stack([cos2, sin2], 1), np.stack([-sin2, cos2], 1)])
    two = two.reshape(2, owners, rows, 2, LANES).transpose(1, 0, 2, 3, 4)
    second = two.reshape(2 * LANES, 2 * LANES)
    pick = np.einsum("ia,jb->ijab", np.eye(inputs), np.eye(inputs))
    pick = np.repeat(pick[:, :, None], rows, axis=2)
    pick = pick.reshape(inputs * inputs * rows, inputs * inputs)
    return (
        jnp.asarray(first, jnp.bfloat16),
        jnp.asarray(twist_cos, jnp.float32),
        jnp.asarray(twist_sin, jnp.float32),
        jnp.asarray(second, jnp.bfloat16),
        jnp.asarray(pick, jnp.bfloat16),
    )


def correlator(
    stations, cores, stacked, proto, first, twist_cos, twist_sin, second, pick, out,
    held, inner, spec, recv, panel, send_sem, recv_sem, own_sem,
):
    owners = stations * cores
    local_inputs = stacked.shape[1]
    tap_count, q_count = proto.shape[:2]
    blocks = held.shape[0]
    spectra_here = blocks * SUB
    inputs = stations * local_inputs
    per_group = q_count // GROUPS
    stn, core = lax.axis_index("stn"), lax.axis_index("chan")
    me = stn * cores + core

    barrier = pltpu.get_barrier_semaphore()

    def greet(r, carry):
        peer = lax.rem(me + r, owners)
        pl.semaphore_signal(
            barrier, inc=1, device_id={"stn": peer // cores, "chan": lax.rem(peer, cores)},
            device_id_type=MESH,
        )
        return carry

    lax.fori_loop(1, owners, greet, 0)

    def copy_out(i, group, peer):
        part = pl.ds(group * per_group, per_group)
        return pltpu.make_async_remote_copy(
            src_ref=spec.at[i, peer, part],
            dst_ref=recv.at[core, stn * local_inputs + i, part],
            send_sem=send_sem.at[i, group, peer],
            recv_sem=recv_sem.at[i, group, me],
            device_id={"stn": peer // cores, "chan": lax.rem(peer, cores)},
            device_id_type=MESH,
        )

    def copy_in(i, group, peer):
        part = pl.ds(group * per_group, per_group)
        return pltpu.make_async_remote_copy(
            src_ref=spec.at[i, peer, part],
            dst_ref=recv.at[lax.rem(peer, cores), peer // cores * local_inputs + i, part],
            send_sem=send_sem.at[i, group, peer],
            recv_sem=recv_sem.at[i, group, peer],
            device_id={"stn": peer // cores, "chan": lax.rem(peer, cores)},
            device_id_type=MESH,
        )

    def copy_own(i, group):
        part = pl.ds(group * per_group, per_group)
        return pltpu.make_async_copy(
            spec.at[i, me, part], recv.at[core, stn * local_inputs + i, part], own_sem.at[i, group]
        )

    halves = q_count // PACK
    for i in range(local_inputs):

        def filter_block(n, carry):
            block = n // (2 * halves)
            c = lax.rem(n // halves, 2)
            rows = pl.ds(pl.multiple_of(lax.rem(n, halves) * PACK, PACK), PACK)
            sums = [None] * SUB
            for f in range(SUB + tap_count - 1):
                frame = stacked[c, i, block * SUB + f, rows, :].astype(jnp.float32)
                for s in range(max(0, f - tap_count + 1), min(SUB, f + 1)):
                    term = proto[f - s, rows, :] * frame
                    sums[s] = term if sums[s] is None else sums[s] + term
            for s in range(SUB):
                held[block, s, c, rows, :] = sums[s].astype(jnp.bfloat16)
            return carry

        lax.fori_loop(0, blocks * 2 * halves, filter_block, 0)

        def first_stage(pair, carry):
            wide = SUB * 2 * q_count
            x = jnp.concatenate(
                [held[2 * pair].reshape(wide, LANES), held[2 * pair + 1].reshape(wide, LANES)], axis=1
            )
            g = jnp.dot(first[...], x, preferred_element_type=jnp.float32)
            g = g.reshape(2, q_count, SUB, 2 * LANES)
            g = jnp.concatenate([g[..., :LANES], g[..., LANES:]], axis=2)
            cos = twist_cos[...][:, None, :]
            sin = twist_sin[...][:, None, :]
            rows = pl.ds(pl.multiple_of(pair * PACK, PACK), PACK)
            inner[:, rows, pl.ds(0, LANES)] = (g[0] * cos + g[1] * sin).astype(jnp.bfloat16)
            inner[:, rows, pl.ds(LANES, LANES)] = (g[1] * cos - g[0] * sin).astype(jnp.bfloat16)
            return carry

        lax.fori_loop(0, blocks // 2, first_stage, 0)

        if i == 0:
            pl.semaphore_wait(barrier, owners - 1)

        def second_stage(group, carry):
            def one_pair(n, inside):
                k = group * per_group + 2 * n
                z = inner[pl.ds(k, 2)].reshape(2 * spectra_here, 2 * LANES)
                made = lax.dot_general(
                    second[...], z, (((1,), (1,)), ((), ())), preferred_element_type=jnp.float32
                ).astype(jnp.bfloat16)
                for e in range(2):
                    piece = made[:, e * spectra_here : (e + 1) * spectra_here]
                    spec[i, :, k + e] = piece.reshape(owners, PACK, spectra_here)
                return inside

            lax.fori_loop(0, per_group // 2, one_pair, 0)

            def send(r, inside):
                side = 1 - 2 * lax.rem(r, 2)
                peer = lax.rem(me + owners // 2 + side * ((r + 1) // 2) + owners, owners)
                copy_out(i, group, peer).start()
                return inside

            lax.fori_loop(0, owners - 1, send, 0)
            copy_own(i, group).start()
            return carry

        lax.fori_loop(0, GROUPS, second_stage, 0)

    row = lax.broadcasted_iota(jnp.int32, (SUB, LANES), 0)
    col = lax.broadcasted_iota(jnp.int32, (SUB, LANES), 1)
    same = (lax.rem(col, SUB) == row).astype(jnp.float32) * (1.0 / (cores * spectra_here))

    def correlate(group, carry):
        for i in range(local_inputs):

            def arrived(r, inside):
                copy_in(i, group, lax.rem(me + r, owners)).wait_recv()
                return inside

            lax.fori_loop(1, owners, arrived, 0)
            copy_own(i, group).wait()

        def one(n, inside):
            k = group * per_group + n
            left, right = [], []
            for h in range(cores):
                a = recv[h, :, k].astype(jnp.float32).reshape(inputs, 2, SUB, spectra_here)
                re = a[:, 0].reshape(inputs * SUB, spectra_here)
                im = a[:, 1].reshape(inputs * SUB, spectra_here)
                left.append(jnp.concatenate([re, im], axis=0).astype(jnp.bfloat16))
                left.append(jnp.concatenate([im, -re], axis=0).astype(jnp.bfloat16))
                right.append(re.astype(jnp.bfloat16))
                right.append(im.astype(jnp.bfloat16))
            v = lax.dot_general(
                jnp.concatenate(left, axis=1), jnp.concatenate(right, axis=1),
                (((1,), (1,)), ((), ())), preferred_element_type=jnp.float32,
            ).reshape(2, inputs, SUB, LANES)
            for c in range(2):
                for j in range(inputs):
                    panel[c, n, :, pl.ds(j * LANES, LANES)] = v[c, j] * same
            return inside

        lax.fori_loop(0, per_group, one, 0)
        flat = panel[...].reshape(2 * per_group * SUB, inputs * LANES)
        high = flat.astype(jnp.bfloat16)
        low = (flat - high.astype(jnp.float32)).astype(jnp.bfloat16)
        total = jnp.dot(high, pick[...], preferred_element_type=jnp.float32) + jnp.dot(
            low, pick[...], preferred_element_type=jnp.float32
        )
        total = total.reshape(2, per_group, SUB, inputs * inputs)
        out[:, pl.ds(group * per_group, per_group)] = total
        return carry

    lax.fori_loop(0, GROUPS, correlate, 0)

    def drain(n, carry):
        i, group, r = n // (GROUPS * (owners - 1)), lax.rem(n // (owners - 1), GROUPS), lax.rem(n, owners - 1)
        copy_out(i, group, lax.rem(me + 1 + r, owners)).wait_send()
        return carry

    lax.fori_loop(0, local_inputs * GROUPS * (owners - 1), drain, 0)


def kernel_fits(voltage, prototype, owners, inputs):
    spectra_here = voltage.shape[2] // prototype.shape[1]
    channels = prototype.shape[1]
    return (
        channels == 32 * LANES
        and spectra_here == LANES
        and channels // owners == 32 * SUB
        and inputs * SUB == LANES
    )


def shards(voltage, earlier_samples, prototype):
    components, local_inputs, samples = voltage.shape
    tap_count, channels = prototype.shape
    stations, cores = lax.axis_size("stn"), lax.axis_size("chan")
    owners, inputs = stations * cores, stations * local_inputs
    if not kernel_fits(voltage, prototype, owners, inputs):
        return general_shards(voltage, earlier_samples, prototype)
    spectra_here = samples // channels
    q_count = channels // LANES
    rows = channels // owners // q_count
    tail = voltage[:, :, samples - (tap_count - 1) * channels :]
    passed = passed_along(tail, "chan", 1)
    history = jnp.where(lax.axis_index("chan") == 0, earlier_samples, passed)
    stacked = jnp.concatenate(
        [
            history.reshape(components, local_inputs, tap_count - 1, q_count, LANES),
            voltage.reshape(components, local_inputs, spectra_here, q_count, LANES),
        ],
        axis=2,
    )
    proto = prototype.reshape(tap_count, q_count, LANES)
    consts = tables(channels, owners, rows, inputs)
    vmem = pl.BlockSpec(memory_space=pltpu.VMEM)
    blocks = spectra_here // SUB
    made = pl.pallas_call(
        functools.partial(correlator, stations, cores),
        out_shape=jax.ShapeDtypeStruct((components, q_count, rows, inputs * inputs), jnp.float32),
        in_specs=[vmem] * 7,
        out_specs=vmem,
        scratch_shapes=[
            pltpu.VMEM((blocks, SUB, components, q_count, LANES), jnp.bfloat16),
            pltpu.VMEM((q_count, spectra_here, 2 * LANES), jnp.bfloat16),
            pltpu.VMEM((local_inputs, owners, q_count, PACK, spectra_here), jnp.bfloat16),
            pltpu.VMEM((cores, inputs, q_count, PACK, spectra_here), jnp.bfloat16),
            pltpu.VMEM((components, q_count // GROUPS, SUB, inputs * LANES), jnp.float32),
            pltpu.SemaphoreType.DMA((local_inputs, GROUPS, owners)),
            pltpu.SemaphoreType.DMA((local_inputs, GROUPS, owners)),
            pltpu.SemaphoreType.DMA((local_inputs, GROUPS)),
        ],
        compiler_params=pltpu.CompilerParams(
            collective_id=0, has_side_effects=True, vmem_limit_bytes=48 * 1024 * 1024
        ),
    )(stacked, proto, *consts)
    made = jnp.transpose(made, (0, 2, 1, 3))
    return made.reshape(components, rows * q_count, inputs * inputs)


def solution(mesh):
    in_specs = (P(None, ("grp", "stn"), "chan"), P(None, ("grp", "stn"), None), P())
    out_specs = P(None, ("grp", "stn", "chan"), None)
    return jax.shard_map(shards, mesh=mesh, in_specs=in_specs, out_specs=out_specs, check_vma=False)
```

```python
import functools
import math

import jax
import jax.numpy as jnp
import numpy as np
from jax import lax
from jax.experimental import pallas as pl
from jax.experimental.pallas import tpu as pltpu
from jax.sharding import PartitionSpec as P

FA = 64
LANES = 128
SUB = 8
PACK = 16
GROUPS = 4
CHUNKS = 2
MESH = pl.DeviceIdType.MESH


def passed_along(block, axis, distance):
    devices = range(lax.axis_size(axis))
    route = [(i - distance, i) for i in devices if i - distance in devices]
    return lax.ppermute(block, axis, route)


def small_tables(length):
    row_index = lax.broadcasted_iota(jnp.int32, (length, length), 0)
    col_index = lax.broadcasted_iota(jnp.int32, (length, length), 1)
    phase_angle = (row_index * col_index % length).astype(jnp.float32) * (2.0 * math.pi / length)
    return (jnp.cos(phase_angle).astype(jnp.bfloat16), jnp.sin(phase_angle).astype(jnp.bfloat16))


def general_shards(voltage, earlier_samples, prototype):
    components, local_inputs, samples = voltage.shape
    tap_count, channels = prototype.shape
    spectra_here = samples // channels
    frames = voltage.reshape(components, local_inputs, spectra_here, channels)
    tail_frames = frames[:, :, spectra_here - (tap_count - 1) :]
    passed = passed_along(tail_frames, "chan", 1)
    earlier = earlier_samples.reshape(components, local_inputs, tap_count - 1, channels)
    leading = lax.axis_index("chan") == 0
    history = jnp.where(leading, earlier, passed)
    stacked = jnp.concatenate([history, frames], axis=2)
    filtered = jnp.zeros((components, local_inputs, spectra_here, channels), jnp.float32)
    for tap_number in range(tap_count):
        window_frames = stacked[:, :, tap_number : tap_number + spectra_here].astype(jnp.float32)
        filtered = filtered + prototype[tap_number] * window_frames
    half_rows = local_inputs * spectra_here
    first_factor = FA
    second_factor = channels // first_factor
    factored = filtered.astype(jnp.bfloat16).reshape(
        components, half_rows, first_factor, second_factor
    )
    first_cos, first_sin = small_tables(first_factor)
    second_cos, second_sin = small_tables(second_factor)
    with_cos = jnp.einsum("crab,ak->crkb", factored, first_cos, preferred_element_type=jnp.float32)
    with_sin = jnp.einsum("crab,ak->crkb", factored, first_sin, preferred_element_type=jnp.float32)
    g_real = with_cos[0] + with_sin[1]
    g_imag = with_cos[1] - with_sin[0]
    row_k = lax.broadcasted_iota(jnp.int32, (first_factor, second_factor), 0)
    col_b = lax.broadcasted_iota(jnp.int32, (first_factor, second_factor), 1)
    twist = (row_k * col_b % channels).astype(jnp.float32) * (2.0 * math.pi / channels)
    twist_cos = jnp.cos(twist)
    twist_sin = jnp.sin(twist)
    inner = jnp.stack(
        [g_real * twist_cos + g_imag * twist_sin, g_imag * twist_cos - g_real * twist_sin]
    ).astype(jnp.bfloat16)
    second_a = jnp.einsum("crkb,bm->crkm", inner, second_cos, preferred_element_type=jnp.float32)
    second_b = jnp.einsum("crkb,bm->crkm", inner, second_sin, preferred_element_type=jnp.float32)
    scale_factor = channels ** (-0.5)
    real_part = (second_a[0] + second_b[1]) * scale_factor
    imag_part = (second_a[1] - second_b[0]) * scale_factor
    ordered = jnp.transpose(jnp.stack([real_part, imag_part]), (0, 1, 3, 2))
    spectra = ordered.astype(jnp.bfloat16).reshape(components, local_inputs, spectra_here, channels)
    station_count = lax.axis_size("stn")
    core_count = lax.axis_size("chan")
    owners = station_count * core_count
    owned = channels // owners
    shaped = spectra.reshape(components, local_inputs, spectra_here, owners, owned)
    moved = lax.all_to_all(shaped, ("stn", "chan"), split_axis=3, concat_axis=3, tiled=True)
    moved = moved.reshape(components, local_inputs, spectra_here, station_count, core_count, owned)
    moved = jnp.transpose(moved, (0, 3, 1, 4, 2, 5)).reshape(
        components, station_count * local_inputs, core_count * spectra_here, owned
    )
    all_inputs = moved.shape[1]
    spectra_total = moved.shape[2]
    products = jnp.einsum("xisc,yjsc->xycij", moved, moved, preferred_element_type=jnp.float32)
    real_sum = products[0, 0] + products[1, 1]
    imag_sum = products[1, 0] - products[0, 1]
    averaged = jnp.stack([real_sum, imag_sum]) / spectra_total
    return averaged.reshape(components, owned, all_inputs * all_inputs)


def tables(channels, owners, rows, inputs):
    q_count = channels // LANES
    q = np.arange(q_count)
    lane = np.arange(LANES)
    ang1 = 2.0 * np.pi * (np.outer(q, q) % q_count) / q_count
    cos1, sin1 = np.cos(ang1), np.sin(ang1)
    one = np.block([[cos1, sin1], [-sin1, cos1]])
    one = one.reshape(2, q_count, 2, q_count)
    eye = np.eye(SUB)
    both = np.eye(2)
    first = np.einsum("ckdq,st,ij->ickstdqj", one, eye, both)
    first = first.reshape(4 * q_count * SUB, 4 * q_count * SUB)
    ang = 2.0 * np.pi * (np.outer(q, lane) % channels) / channels
    twist_cos, twist_sin = np.cos(ang), np.sin(ang)
    ang2 = 2.0 * np.pi * (np.outer(lane, lane) % LANES) / LANES
    scale = channels ** -0.5
    cos2, sin2 = np.cos(ang2) * scale, np.sin(ang2) * scale
    two = np.stack([np.stack([cos2, sin2], 1), np.stack([-sin2, cos2], 1)])
    two = two.reshape(2, owners, rows, 2, LANES).transpose(1, 0, 2, 3, 4)
    second = two.reshape(2 * LANES, 2 * LANES)
    pick = np.einsum("ia,jb->ijab", np.eye(inputs), np.eye(inputs))
    pick = np.repeat(pick[:, :, None], rows, axis=2)
    pick = pick.reshape(inputs * inputs * rows, inputs * inputs)
    return (
        jnp.asarray(first, jnp.bfloat16),
        jnp.asarray(twist_cos, jnp.float32),
        jnp.asarray(twist_sin, jnp.float32),
        jnp.asarray(second, jnp.bfloat16),
        jnp.asarray(pick, jnp.bfloat16),
    )


def correlator(
    stations, cores, voltage, earlier, first_hbm, pick_hbm, proto, twist_cos, twist_sin, second, out,
    stream, first, pick, held, inner, spec, recv, panel, send_sem, recv_sem, own_sem, load_sem, halo_sem,
):
    owners = stations * cores
    local_inputs = 2
    tap_count, frame_rows = proto.shape[:2]
    q_count = frame_rows // local_inputs
    blocks = held.shape[0]
    spectra_chunk = blocks * SUB
    spectra_here = CHUNKS * spectra_chunk
    inputs = stations * local_inputs
    per_group = q_count // GROUPS
    stn, core = lax.axis_index("stn"), lax.axis_index("chan")
    me = stn * cores + core
    lead = tap_count - 1

    barrier = pltpu.get_barrier_semaphore()

    def greet(r, carry):
        peer = lax.rem(me + r, owners)
        pl.semaphore_signal(
            barrier, inc=1, device_id={"stn": peer // cores, "chan": lax.rem(peer, cores)},
            device_id_type=MESH,
        )
        return carry

    def load(c, begin, end, sem):
        count = (end - begin) * frame_rows
        return pltpu.make_async_copy(
            voltage.at[c, pl.ds(begin * frame_rows, count)],
            stream.at[c, pl.ds((begin + lead) * frame_rows, count)],
            load_sem.at[sem],
        )

    split = spectra_here - spectra_chunk - lead
    late = [load(c, split, spectra_here, c) for c in range(2)]
    early = [load(c, 0, split, 2 + c) for c in range(2)]
    get_first = pltpu.make_async_copy(first_hbm, first, load_sem.at[4])
    get_pick = pltpu.make_async_copy(pick_hbm, pick, load_sem.at[5])
    history = stream.at[:, pl.ds(0, lead * frame_rows)]
    get_earlier = pltpu.make_async_copy(earlier, history, load_sem.at[6])
    halo = pltpu.make_async_remote_copy(
        src_ref=voltage.at[:, pl.ds((spectra_here - lead) * frame_rows, lead * frame_rows)],
        dst_ref=history,
        send_sem=halo_sem.at[0],
        recv_sem=halo_sem.at[1],
        device_id={"stn": stn, "chan": lax.rem(core + 1, cores)},
        device_id_type=MESH,
    )
    for copy in late:
        copy.start()
    get_first.start()
    lax.fori_loop(1, owners, greet, 0)
    for copy in early:
        copy.start()

    @pl.when(core == 0)
    def _():
        get_earlier.start()

    get_pick.start()

    def copy_out(i, group, peer):
        part = pl.ds(group * per_group, per_group)
        return pltpu.make_async_remote_copy(
            src_ref=spec.at[i, peer, part],
            dst_ref=recv.at[core, i, stn, part],
            send_sem=send_sem.at[i, group, peer],
            recv_sem=recv_sem.at[i, group, me],
            device_id={"stn": peer // cores, "chan": lax.rem(peer, cores)},
            device_id_type=MESH,
        )

    def copy_in(i, group, peer):
        part = pl.ds(group * per_group, per_group)
        return pltpu.make_async_remote_copy(
            src_ref=spec.at[i, peer, part],
            dst_ref=recv.at[lax.rem(peer, cores), i, peer // cores, part],
            send_sem=send_sem.at[i, group, peer],
            recv_sem=recv_sem.at[i, group, peer],
            device_id={"stn": peer // cores, "chan": lax.rem(peer, cores)},
            device_id_type=MESH,
        )

    def copy_own(i, group):
        part = pl.ds(group * per_group, per_group)
        return pltpu.make_async_copy(
            spec.at[i, me, part], recv.at[core, i, stn, part], own_sem.at[i, group]
        )

    pieces = frame_rows // PACK
    for i in range(CHUNKS):
        start = spectra_here - (i + 1) * spectra_chunk
        if i == 0:
            for copy in late:
                copy.wait()
        else:
            for copy in early:
                copy.wait()

            @pl.when(core == 0)
            def _():
                get_earlier.wait()

            @pl.when(core > 0)
            def _():
                halo.wait_recv()

        def filter_block(n, carry):
            block = n // (2 * pieces)
            c = lax.rem(n // pieces, 2)
            offset = lax.rem(n, pieces) * PACK
            rows = pl.ds(pl.multiple_of(offset, PACK), PACK)
            sums = [None] * SUB
            for f in range(SUB + lead):
                place = (start + block * SUB + f) * frame_rows + offset
                frame = stream[c, pl.ds(pl.multiple_of(place, PACK), PACK), :].astype(jnp.float32)
                for s in range(max(0, f - lead), min(SUB, f + 1)):
                    term = proto[f - s, rows, :] * frame
                    sums[s] = term if sums[s] is None else sums[s] + term
            for s in range(SUB):
                held[block, s, c, rows, :] = sums[s].astype(jnp.bfloat16)
            return carry

        lax.fori_loop(0, blocks * 2 * pieces, filter_block, 0)
        if i == 0:
            get_first.wait()
            pl.semaphore_wait(barrier, owners - 1)

            @pl.when(core < cores - 1)
            def _():
                halo.start()

        half = 2 * q_count * SUB

        def first_stage(n, carry):
            pair, part = n // local_inputs, lax.rem(n, local_inputs)
            wide = SUB * 2 * frame_rows
            x = jnp.concatenate(
                [held[2 * pair].reshape(wide, LANES), held[2 * pair + 1].reshape(wide, LANES)], axis=1
            )
            weights = first[pl.ds(pl.multiple_of(part * half, half), half), :]
            g = jnp.dot(weights, x, preferred_element_type=jnp.float32)
            g = g.reshape(2, q_count, SUB, 2 * LANES)
            g = jnp.concatenate([g[..., :LANES], g[..., LANES:]], axis=2)
            cos = twist_cos[...][:, None, :]
            sin = twist_sin[...][:, None, :]
            rows = pl.ds(pl.multiple_of(part * spectra_chunk + pair * PACK, PACK), PACK)
            inner[:, rows, pl.ds(0, LANES)] = (g[0] * cos + g[1] * sin).astype(jnp.bfloat16)
            inner[:, rows, pl.ds(LANES, LANES)] = (g[1] * cos - g[0] * sin).astype(jnp.bfloat16)
            return carry

        lax.fori_loop(0, blocks // 2 * local_inputs, first_stage, 0)

        def second_stage(group, carry):
            def one_pair(n, inside):
                k = group * per_group + 2 * n
                z = inner[pl.ds(k, 2)].reshape(2 * LANES, 2 * LANES)
                made = lax.dot_general(
                    second[...], z, (((1,), (1,)), ((), ())), preferred_element_type=jnp.float32
                ).astype(jnp.bfloat16)
                for e in range(2):
                    piece = made[:, e * LANES : (e + 1) * LANES]
                    spec[i, :, k + e] = piece.reshape(owners, PACK, LANES)
                return inside

            lax.fori_loop(0, per_group // 2, one_pair, 0)

            def send(r, inside):
                side = 1 - 2 * lax.rem(r, 2)
                peer = lax.rem(me + owners // 2 + side * ((r + 1) // 2) + owners, owners)
                copy_out(i, group, peer).start()
                return inside

            lax.fori_loop(0, owners - 1, send, 0)
            copy_own(i, group).start()
            return carry

        lax.fori_loop(0, GROUPS, second_stage, 0)

    get_pick.wait()
    row = lax.broadcasted_iota(jnp.int32, (SUB, LANES), 0)
    col = lax.broadcasted_iota(jnp.int32, (SUB, LANES), 1)
    same = (lax.rem(col, SUB) == row).astype(jnp.float32) * (1.0 / (cores * spectra_here))

    lower = lax.broadcasted_iota(jnp.int32, (SUB * inputs, LANES), 1) < spectra_chunk

    def correlate(group, carry):
        for i in range(CHUNKS):

            def arrived(r, inside):
                copy_in(i, group, lax.rem(me + r, owners)).wait_recv()
                return inside

            lax.fori_loop(1, owners, arrived, 0)
            copy_own(i, group).wait()

        def one(n, inside):
            k = group * per_group + n
            left, right = [], []
            for h in range(cores):
                a = recv[h, 0, :, k].astype(jnp.float32).reshape(inputs * SUB, LANES)
                b = recv[h, 1, :, k].astype(jnp.float32).reshape(inputs * SUB, LANES)
                one_in = jnp.where(lower, a, pltpu.roll(b, spectra_chunk, 1))
                two_in = jnp.where(lower, pltpu.roll(a, spectra_chunk, 1), b)
                one_in = one_in.reshape(stations, 2, SUB, LANES)
                two_in = two_in.reshape(stations, 2, SUB, LANES)
                both = jnp.stack([one_in, two_in], axis=1)
                re = both[:, :, 0].reshape(inputs * SUB, LANES)
                im = both[:, :, 1].reshape(inputs * SUB, LANES)
                left.append(jnp.concatenate([re, im], axis=0).astype(jnp.bfloat16))
                left.append(jnp.concatenate([im, -re], axis=0).astype(jnp.bfloat16))
                right.append(re.astype(jnp.bfloat16))
                right.append(im.astype(jnp.bfloat16))
            v = lax.dot_general(
                jnp.concatenate(left, axis=1), jnp.concatenate(right, axis=1),
                (((1,), (1,)), ((), ())), preferred_element_type=jnp.float32,
            ).reshape(2, inputs, SUB, LANES)
            for c in range(2):
                for j in range(inputs):
                    panel[c, n, :, pl.ds(j * LANES, LANES)] = v[c, j] * same
            return inside

        lax.fori_loop(0, per_group, one, 0)
        flat = panel[...].reshape(2 * per_group * SUB, inputs * LANES)
        high = flat.astype(jnp.bfloat16)
        low = (flat - high.astype(jnp.float32)).astype(jnp.bfloat16)
        total = jnp.dot(high, pick[...], preferred_element_type=jnp.float32) + jnp.dot(
            low, pick[...], preferred_element_type=jnp.float32
        )
        total = total.reshape(2, per_group, SUB, inputs * inputs)
        out[:, pl.ds(group * per_group, per_group)] = total
        return carry

    lax.fori_loop(0, GROUPS, correlate, 0)

    def drain(n, carry):
        i, group, r = n // (GROUPS * (owners - 1)), lax.rem(n // (owners - 1), GROUPS), lax.rem(n, owners - 1)
        copy_out(i, group, lax.rem(me + 1 + r, owners)).wait_send()
        return carry

    lax.fori_loop(0, CHUNKS * GROUPS * (owners - 1), drain, 0)

    @pl.when(core < cores - 1)
    def _():
        halo.wait_send()


def kernel_fits(voltage, prototype, stations, cores, inputs):
    owners = stations * cores
    spectra_here = voltage.shape[2] // prototype.shape[1]
    channels = prototype.shape[1]
    return (
        channels == 32 * LANES
        and spectra_here == LANES
        and channels // owners == 32 * SUB
        and inputs * SUB == LANES
        and inputs == 2 * stations
        and cores == 2
    )


def shards(voltage, earlier_samples, prototype):
    components, local_inputs, samples = voltage.shape
    tap_count, channels = prototype.shape
    stations, cores = lax.axis_size("stn"), lax.axis_size("chan")
    owners, inputs = stations * cores, stations * local_inputs
    if not kernel_fits(voltage, prototype, stations, cores, inputs):
        return general_shards(voltage, earlier_samples, prototype)
    spectra_here = samples // channels
    q_count = channels // LANES
    rows = channels // owners // q_count

    def by_rows(array):
        array = array.reshape(components, local_inputs, -1, LANES)
        return jnp.transpose(array, (0, 2, 1, 3)).reshape(components, -1, LANES)

    proto = jnp.repeat(prototype.reshape(tap_count, q_count, LANES), local_inputs, axis=1)
    first, twist_cos, twist_sin, second, pick = tables(channels, owners, rows, inputs)
    vmem = pl.BlockSpec(memory_space=pltpu.VMEM)
    anywhere = pl.BlockSpec(memory_space=pl.ANY)
    frame_rows = local_inputs * q_count
    blocks = spectra_here // CHUNKS // SUB
    made = pl.pallas_call(
        functools.partial(correlator, stations, cores),
        out_shape=jax.ShapeDtypeStruct((components, q_count, rows, inputs * inputs), jnp.float32),
        in_specs=[anywhere] * 4 + [vmem] * 4,
        out_specs=vmem,
        scratch_shapes=[
            pltpu.VMEM((components, (spectra_here + tap_count - 1) * frame_rows, LANES), jnp.bfloat16),
            pltpu.VMEM(first.shape, jnp.bfloat16),
            pltpu.VMEM(pick.shape, jnp.bfloat16),
            pltpu.VMEM((blocks, SUB, components, frame_rows, LANES), jnp.bfloat16),
            pltpu.VMEM((q_count, LANES, 2 * LANES), jnp.bfloat16),
            pltpu.VMEM((CHUNKS, owners, q_count, PACK, LANES), jnp.bfloat16),
            pltpu.VMEM((cores, CHUNKS, stations, q_count, PACK, LANES), jnp.bfloat16),
            pltpu.VMEM((components, q_count // GROUPS, SUB, inputs * LANES), jnp.float32),
            pltpu.SemaphoreType.DMA((CHUNKS, GROUPS, owners)),
            pltpu.SemaphoreType.DMA((CHUNKS, GROUPS, owners)),
            pltpu.SemaphoreType.DMA((CHUNKS, GROUPS)),
            pltpu.SemaphoreType.DMA((7,)),
            pltpu.SemaphoreType.DMA((2,)),
        ],
        compiler_params=pltpu.CompilerParams(
            collective_id=0, has_side_effects=True, vmem_limit_bytes=58 * 1024 * 1024
        ),
    )(
        by_rows(voltage), by_rows(earlier_samples), first, pick, proto, twist_cos, twist_sin, second
    )
    made = jnp.transpose(made, (0, 2, 1, 3))
    return made.reshape(components, rows * q_count, inputs * inputs)


def solution(mesh):
    in_specs = (P(None, ("grp", "stn"), "chan"), P(None, ("grp", "stn"), None), P())
    out_specs = P(None, ("grp", "stn", "chan"), None)
    return jax.shard_map(shards, mesh=mesh, in_specs=in_specs, out_specs=out_specs, check_vma=False)
```

```python
import functools
import math

import jax
import jax.numpy as jnp
import numpy as np
from jax import lax
from jax.experimental import pallas as pl
from jax.experimental.pallas import tpu as pltpu
from jax.sharding import PartitionSpec as P

FA = 64
LANES = 128
SUB = 8
PACK = 16
GROUPS = 4
CHUNKS = 2
MESH = pl.DeviceIdType.MESH


def passed_along(block, axis, distance):
    devices = range(lax.axis_size(axis))
    route = [(i - distance, i) for i in devices if i - distance in devices]
    return lax.ppermute(block, axis, route)


def small_tables(length):
    row_index = lax.broadcasted_iota(jnp.int32, (length, length), 0)
    col_index = lax.broadcasted_iota(jnp.int32, (length, length), 1)
    phase_angle = (row_index * col_index % length).astype(jnp.float32) * (2.0 * math.pi / length)
    return (jnp.cos(phase_angle).astype(jnp.bfloat16), jnp.sin(phase_angle).astype(jnp.bfloat16))


def general_shards(voltage, earlier_samples, prototype):
    components, local_inputs, samples = voltage.shape
    tap_count, channels = prototype.shape
    spectra_here = samples // channels
    frames = voltage.reshape(components, local_inputs, spectra_here, channels)
    tail_frames = frames[:, :, spectra_here - (tap_count - 1) :]
    passed = passed_along(tail_frames, "chan", 1)
    earlier = earlier_samples.reshape(components, local_inputs, tap_count - 1, channels)
    leading = lax.axis_index("chan") == 0
    history = jnp.where(leading, earlier, passed)
    stacked = jnp.concatenate([history, frames], axis=2)
    filtered = jnp.zeros((components, local_inputs, spectra_here, channels), jnp.float32)
    for tap_number in range(tap_count):
        window_frames = stacked[:, :, tap_number : tap_number + spectra_here].astype(jnp.float32)
        filtered = filtered + prototype[tap_number] * window_frames
    half_rows = local_inputs * spectra_here
    first_factor = FA
    second_factor = channels // first_factor
    factored = filtered.astype(jnp.bfloat16).reshape(
        components, half_rows, first_factor, second_factor
    )
    first_cos, first_sin = small_tables(first_factor)
    second_cos, second_sin = small_tables(second_factor)
    with_cos = jnp.einsum("crab,ak->crkb", factored, first_cos, preferred_element_type=jnp.float32)
    with_sin = jnp.einsum("crab,ak->crkb", factored, first_sin, preferred_element_type=jnp.float32)
    g_real = with_cos[0] + with_sin[1]
    g_imag = with_cos[1] - with_sin[0]
    row_k = lax.broadcasted_iota(jnp.int32, (first_factor, second_factor), 0)
    col_b = lax.broadcasted_iota(jnp.int32, (first_factor, second_factor), 1)
    twist = (row_k * col_b % channels).astype(jnp.float32) * (2.0 * math.pi / channels)
    twist_cos = jnp.cos(twist)
    twist_sin = jnp.sin(twist)
    inner = jnp.stack(
        [g_real * twist_cos + g_imag * twist_sin, g_imag * twist_cos - g_real * twist_sin]
    ).astype(jnp.bfloat16)
    second_a = jnp.einsum("crkb,bm->crkm", inner, second_cos, preferred_element_type=jnp.float32)
    second_b = jnp.einsum("crkb,bm->crkm", inner, second_sin, preferred_element_type=jnp.float32)
    scale_factor = channels ** (-0.5)
    real_part = (second_a[0] + second_b[1]) * scale_factor
    imag_part = (second_a[1] - second_b[0]) * scale_factor
    ordered = jnp.transpose(jnp.stack([real_part, imag_part]), (0, 1, 3, 2))
    spectra = ordered.astype(jnp.bfloat16).reshape(components, local_inputs, spectra_here, channels)
    station_count = lax.axis_size("stn")
    core_count = lax.axis_size("chan")
    owners = station_count * core_count
    owned = channels // owners
    shaped = spectra.reshape(components, local_inputs, spectra_here, owners, owned)
    moved = lax.all_to_all(shaped, ("stn", "chan"), split_axis=3, concat_axis=3, tiled=True)
    moved = moved.reshape(components, local_inputs, spectra_here, station_count, core_count, owned)
    moved = jnp.transpose(moved, (0, 3, 1, 4, 2, 5)).reshape(
        components, station_count * local_inputs, core_count * spectra_here, owned
    )
    all_inputs = moved.shape[1]
    spectra_total = moved.shape[2]
    products = jnp.einsum("xisc,yjsc->xycij", moved, moved, preferred_element_type=jnp.float32)
    real_sum = products[0, 0] + products[1, 1]
    imag_sum = products[1, 0] - products[0, 1]
    averaged = jnp.stack([real_sum, imag_sum]) / spectra_total
    return averaged.reshape(components, owned, all_inputs * all_inputs)


def tables(channels, owners, rows, inputs):
    q_count = channels // LANES
    q = np.arange(q_count)
    lane = np.arange(LANES)
    ang1 = 2.0 * np.pi * (np.outer(q, q) % q_count) / q_count
    cos1, sin1 = np.cos(ang1), np.sin(ang1)
    one = np.block([[cos1, sin1], [-sin1, cos1]])
    one = one.reshape(2, q_count, 2, q_count)
    eye = np.eye(SUB)
    both = np.eye(2)
    first = np.einsum("ckdq,st,ij->ickstdqj", one, eye, both)
    first = first.reshape(2, 2, GROUPS, q_count // GROUPS, SUB, -1).transpose(2, 0, 1, 3, 4, 5)
    first = first.reshape(4 * q_count * SUB, 4 * q_count * SUB)
    ang = 2.0 * np.pi * (np.outer(q, lane) % channels) / channels
    twist_cos, twist_sin = np.cos(ang), np.sin(ang)
    ang2 = 2.0 * np.pi * (np.outer(lane, lane) % LANES) / LANES
    scale = channels ** -0.5
    cos2, sin2 = np.cos(ang2) * scale, np.sin(ang2) * scale
    two = np.stack([np.stack([cos2, sin2], 1), np.stack([-sin2, cos2], 1)])
    two = two.reshape(2, owners, rows, 2, LANES).transpose(1, 0, 2, 3, 4)
    second = two.reshape(2 * LANES, 2 * LANES)
    pick = np.einsum("ia,jb->ijab", np.eye(inputs), np.eye(inputs))
    pick = np.repeat(pick[:, :, None], rows, axis=2)
    pick = pick.reshape(inputs * inputs * rows, inputs * inputs)
    return (
        jnp.asarray(first, jnp.bfloat16),
        jnp.asarray(twist_cos, jnp.float32),
        jnp.asarray(twist_sin, jnp.float32),
        jnp.asarray(second, jnp.bfloat16),
        jnp.asarray(pick, jnp.bfloat16),
    )


def correlator(
    stations, cores, voltage, earlier, first_hbm, pick_hbm, coeffs, twist_cos, twist_sin, second, out,
    proto, stream, first, pick, held, inner, spec, recv, panel, send_sem, recv_sem, own_sem, load_sem, halo_sem,
):
    owners = stations * cores
    local_inputs = 2
    tap_count, frame_rows = proto.shape[:2]
    q_count = frame_rows // local_inputs
    blocks = held.shape[0]
    spectra_chunk = blocks * SUB
    spectra_here = CHUNKS * spectra_chunk
    inputs = stations * local_inputs
    per_group = q_count // GROUPS
    stn, core = lax.axis_index("stn"), lax.axis_index("chan")
    me = stn * cores + core
    lead = tap_count - 1

    barrier = pltpu.get_barrier_semaphore()

    def greet(r, carry):
        peer = lax.rem(me + r, owners)
        pl.semaphore_signal(
            barrier, inc=1, device_id={"stn": peer // cores, "chan": lax.rem(peer, cores)},
            device_id_type=MESH,
        )
        return carry

    def load(c, begin, end, sem):
        count = (end - begin) * frame_rows
        return pltpu.make_async_copy(
            voltage.at[c, pl.ds(begin * frame_rows, count)],
            stream.at[c, pl.ds((begin + lead) * frame_rows, count)],
            load_sem.at[sem],
        )

    split = spectra_here - spectra_chunk - lead
    late = [load(c, split, spectra_here, c) for c in range(2)]
    early = [load(c, 0, split, 2 + c) for c in range(2)]
    get_first = pltpu.make_async_copy(first_hbm, first, load_sem.at[4])
    get_pick = pltpu.make_async_copy(pick_hbm, pick, load_sem.at[5])
    history = stream.at[:, pl.ds(0, lead * frame_rows)]
    get_earlier = pltpu.make_async_copy(earlier, history, load_sem.at[6])
    halo = pltpu.make_async_remote_copy(
        src_ref=voltage.at[:, pl.ds((spectra_here - lead) * frame_rows, lead * frame_rows)],
        dst_ref=history,
        send_sem=halo_sem.at[0],
        recv_sem=halo_sem.at[1],
        device_id={"stn": stn, "chan": lax.rem(core + 1, cores)},
        device_id_type=MESH,
    )
    for copy in late:
        copy.start()
    get_first.start()
    lax.fori_loop(1, owners, greet, 0)
    for copy in early:
        copy.start()

    @pl.when(core == 0)
    def _():
        get_earlier.start()

    get_pick.start()

    for q in range(q_count):
        column = coeffs[:, q * LANES : (q + 1) * LANES]
        for i in range(local_inputs):
            proto[:, q * local_inputs + i, :] = column

    def copy_out(i, group, peer):
        part = pl.ds(group * per_group, per_group)
        return pltpu.make_async_remote_copy(
            src_ref=spec.at[i, peer, part],
            dst_ref=recv.at[core, i, stn, part],
            send_sem=send_sem.at[i, group, peer],
            recv_sem=recv_sem.at[i, group, me],
            device_id={"stn": peer // cores, "chan": lax.rem(peer, cores)},
            device_id_type=MESH,
        )

    def copy_in(i, group, peer):
        part = pl.ds(group * per_group, per_group)
        return pltpu.make_async_remote_copy(
            src_ref=spec.at[i, peer, part],
            dst_ref=recv.at[lax.rem(peer, cores), i, peer // cores, part],
            send_sem=send_sem.at[i, group, peer],
            recv_sem=recv_sem.at[i, group, peer],
            device_id={"stn": peer // cores, "chan": lax.rem(peer, cores)},
            device_id_type=MESH,
        )

    def copy_own(i, group):
        part = pl.ds(group * per_group, per_group)
        return pltpu.make_async_copy(
            spec.at[i, me, part], recv.at[core, i, stn, part], own_sem.at[i, group]
        )

    pieces = frame_rows // PACK
    for i in range(CHUNKS):
        start = spectra_here - (i + 1) * spectra_chunk
        if i == 0:
            for copy in late:
                copy.wait()
        else:
            for copy in early:
                copy.wait()

            @pl.when(core == 0)
            def _():
                get_earlier.wait()

            @pl.when(core > 0)
            def _():
                halo.wait_recv()

        def filter_block(n, carry):
            block = n // (2 * pieces)
            c = lax.rem(n // pieces, 2)
            offset = lax.rem(n, pieces) * PACK
            rows = pl.ds(pl.multiple_of(offset, PACK), PACK)
            sums = [None] * SUB
            for f in range(SUB + lead):
                place = (start + block * SUB + f) * frame_rows + offset
                frame = stream[c, pl.ds(pl.multiple_of(place, PACK), PACK), :].astype(jnp.float32)
                for s in range(max(0, f - lead), min(SUB, f + 1)):
                    term = proto[f - s, rows, :] * frame
                    sums[s] = term if sums[s] is None else sums[s] + term
            for s in range(SUB):
                held[block, s, c, rows, :] = sums[s].astype(jnp.bfloat16)
            return carry

        lax.fori_loop(0, blocks * 2 * pieces, filter_block, 0)
        if i == 0:
            get_first.wait()
            pl.semaphore_wait(barrier, owners - 1)

            @pl.when(core < cores - 1)
            def _():
                halo.start()

        count = 4 * per_group * SUB

        def second_stage(group, carry):
            ks = pl.ds(pl.multiple_of(group * per_group, per_group), per_group)

            def first_stage(pair, inside):
                wide = SUB * 2 * frame_rows
                x = jnp.concatenate(
                    [held[2 * pair].reshape(wide, LANES), held[2 * pair + 1].reshape(wide, LANES)], axis=1
                )
                weights = first[pl.ds(pl.multiple_of(group * count, count), count), :]
                g = jnp.dot(weights, x, preferred_element_type=jnp.float32)
                g = g.reshape(local_inputs, 2, per_group, SUB, 2 * LANES)
                g = jnp.concatenate([g[..., :LANES], g[..., LANES:]], axis=3)
                cos = twist_cos[ks, :][:, None, :]
                sin = twist_sin[ks, :][:, None, :]
                for part in range(local_inputs):
                    re, im = g[part, 0], g[part, 1]
                    rows = pl.ds(pl.multiple_of(part * spectra_chunk + pair * PACK, PACK), PACK)
                    inner[ks, rows, pl.ds(0, LANES)] = (re * cos + im * sin).astype(jnp.bfloat16)
                    inner[ks, rows, pl.ds(LANES, LANES)] = (im * cos - re * sin).astype(jnp.bfloat16)
                return inside

            lax.fori_loop(0, blocks // 2, first_stage, 0)

            def one_pair(n, inside):
                k = group * per_group + 2 * n
                z = inner[pl.ds(k, 2)].reshape(2 * LANES, 2 * LANES)
                made = lax.dot_general(
                    second[...], z, (((1,), (1,)), ((), ())), preferred_element_type=jnp.float32
                ).astype(jnp.bfloat16)
                for e in range(2):
                    piece = made[:, e * LANES : (e + 1) * LANES]
                    spec[i, :, k + e] = piece.reshape(owners, PACK, LANES)
                return inside

            lax.fori_loop(0, per_group // 2, one_pair, 0)

            def send(r, inside):
                side = 1 - 2 * lax.rem(r, 2)
                peer = lax.rem(me + owners // 2 + side * ((r + 1) // 2) + owners, owners)
                copy_out(i, group, peer).start()
                return inside

            lax.fori_loop(0, owners - 1, send, 0)
            copy_own(i, group).start()
            return carry

        lax.fori_loop(0, GROUPS, second_stage, 0)

    get_pick.wait()
    row = lax.broadcasted_iota(jnp.int32, (SUB, LANES), 0)
    col = lax.broadcasted_iota(jnp.int32, (SUB, LANES), 1)
    same = (lax.rem(col, SUB) == row).astype(jnp.float32) * (1.0 / (cores * spectra_here))

    lower = lax.broadcasted_iota(jnp.int32, (SUB * inputs, LANES), 1) < spectra_chunk

    def correlate(group, carry):
        for i in range(CHUNKS):

            def arrived(r, inside):
                copy_in(i, group, lax.rem(me + r, owners)).wait_recv()
                return inside

            lax.fori_loop(1, owners, arrived, 0)
            copy_own(i, group).wait()

        def one(n, inside):
            k = group * per_group + n
            left, right = [], []
            for h in range(cores):
                a = recv[h, 0, :, k].astype(jnp.float32).reshape(inputs * SUB, LANES)
                b = recv[h, 1, :, k].astype(jnp.float32).reshape(inputs * SUB, LANES)
                one_in = jnp.where(lower, a, pltpu.roll(b, spectra_chunk, 1))
                two_in = jnp.where(lower, pltpu.roll(a, spectra_chunk, 1), b)
                one_in = one_in.reshape(stations, 2, SUB, LANES)
                two_in = two_in.reshape(stations, 2, SUB, LANES)
                both = jnp.stack([one_in, two_in], axis=1)
                re = both[:, :, 0].reshape(inputs * SUB, LANES)
                im = both[:, :, 1].reshape(inputs * SUB, LANES)
                left.append(jnp.concatenate([re, im], axis=0).astype(jnp.bfloat16))
                left.append(jnp.concatenate([im, -re], axis=0).astype(jnp.bfloat16))
                right.append(re.astype(jnp.bfloat16))
                right.append(im.astype(jnp.bfloat16))
            v = lax.dot_general(
                jnp.concatenate(left, axis=1), jnp.concatenate(right, axis=1),
                (((1,), (1,)), ((), ())), preferred_element_type=jnp.float32,
            ).reshape(2, inputs, SUB, LANES)
            for c in range(2):
                for j in range(inputs):
                    panel[c, n, :, pl.ds(j * LANES, LANES)] = v[c, j] * same
            return inside

        lax.fori_loop(0, per_group, one, 0)
        flat = panel[...].reshape(2 * per_group * SUB, inputs * LANES)
        high = flat.astype(jnp.bfloat16)
        low = (flat - high.astype(jnp.float32)).astype(jnp.bfloat16)
        total = jnp.dot(high, pick[...], preferred_element_type=jnp.float32) + jnp.dot(
            low, pick[...], preferred_element_type=jnp.float32
        )
        total = total.reshape(2, per_group, SUB, inputs * inputs)
        places = pl.ds(pl.multiple_of(group * per_group, per_group), per_group)
        out[:, :, places, :] = jnp.swapaxes(total, 1, 2)
        return carry

    lax.fori_loop(0, GROUPS, correlate, 0)

    def drain(n, carry):
        i, group, r = n // (GROUPS * (owners - 1)), lax.rem(n // (owners - 1), GROUPS), lax.rem(n, owners - 1)
        copy_out(i, group, lax.rem(me + 1 + r, owners)).wait_send()
        return carry

    lax.fori_loop(0, CHUNKS * GROUPS * (owners - 1), drain, 0)

    @pl.when(core < cores - 1)
    def _():
        halo.wait_send()


def kernel_fits(voltage, prototype, stations, cores, inputs):
    owners = stations * cores
    spectra_here = voltage.shape[2] // prototype.shape[1]
    channels = prototype.shape[1]
    return (
        channels == 32 * LANES
        and spectra_here == LANES
        and channels // owners == 32 * SUB
        and inputs * SUB == LANES
        and inputs == 2 * stations
        and cores == 2
    )


def shards(voltage, earlier_samples, prototype):
    components, local_inputs, samples = voltage.shape
    tap_count, channels = prototype.shape
    stations, cores = lax.axis_size("stn"), lax.axis_size("chan")
    owners, inputs = stations * cores, stations * local_inputs
    if not kernel_fits(voltage, prototype, stations, cores, inputs):
        return general_shards(voltage, earlier_samples, prototype)
    spectra_here = samples // channels
    q_count = channels // LANES
    rows = channels // owners // q_count

    def by_rows(array):
        array = array.reshape(components, local_inputs, -1, LANES)
        return jnp.transpose(array, (0, 2, 1, 3)).reshape(components, -1, LANES)

    first, twist_cos, twist_sin, second, pick = tables(channels, owners, rows, inputs)
    vmem = pl.BlockSpec(memory_space=pltpu.VMEM)
    anywhere = pl.BlockSpec(memory_space=pl.ANY)
    frame_rows = local_inputs * q_count
    blocks = spectra_here // CHUNKS // SUB
    made = pl.pallas_call(
        functools.partial(correlator, stations, cores),
        out_shape=jax.ShapeDtypeStruct((components, rows, q_count, inputs * inputs), jnp.float32),
        in_specs=[anywhere] * 4 + [vmem] * 4,
        out_specs=vmem,
        scratch_shapes=[
            pltpu.VMEM((tap_count, frame_rows, LANES), jnp.float32),
            pltpu.VMEM((components, (spectra_here + tap_count - 1) * frame_rows, LANES), jnp.bfloat16),
            pltpu.VMEM(first.shape, jnp.bfloat16),
            pltpu.VMEM(pick.shape, jnp.bfloat16),
            pltpu.VMEM((blocks, SUB, components, frame_rows, LANES), jnp.bfloat16),
            pltpu.VMEM((q_count, LANES, 2 * LANES), jnp.bfloat16),
            pltpu.VMEM((CHUNKS, owners, q_count, PACK, LANES), jnp.bfloat16),
            pltpu.VMEM((cores, CHUNKS, stations, q_count, PACK, LANES), jnp.bfloat16),
            pltpu.VMEM((components, q_count // GROUPS, SUB, inputs * LANES), jnp.float32),
            pltpu.SemaphoreType.DMA((CHUNKS, GROUPS, owners)),
            pltpu.SemaphoreType.DMA((CHUNKS, GROUPS, owners)),
            pltpu.SemaphoreType.DMA((CHUNKS, GROUPS)),
            pltpu.SemaphoreType.DMA((7,)),
            pltpu.SemaphoreType.DMA((2,)),
        ],
        compiler_params=pltpu.CompilerParams(
            collective_id=0, has_side_effects=True, vmem_limit_bytes=58 * 1024 * 1024
        ),
    )(
        by_rows(voltage), by_rows(earlier_samples), first, pick, prototype, twist_cos, twist_sin, second
    )
    return made.reshape(components, rows * q_count, inputs * inputs)


def solution(mesh):
    in_specs = (P(None, ("grp", "stn"), "chan"), P(None, ("grp", "stn"), None), P())
    out_specs = P(None, ("grp", "stn", "chan"), None)
    return jax.shard_map(shards, mesh=mesh, in_specs=in_specs, out_specs=out_specs, check_vma=False)
```
